32 devices in a mesh: member: 4 (over x, core), tile: 8 (over z, y).
Axes of the slice: x: 2, y: 2, z: 4, core: 2. Of those that a mesh axis runs over, the one named last changes fastest.
Arguments:
- upsampled_coarse: bfloat16 [32, 32, 256], P('tile'), may hold values from -6 to 6
- target: bfloat16 [32, 32, 256], P('tile'), may hold values from -6 to 6
- seeds: int32 [8], P('member'), may hold values from 0 to 63
- band_row: int32 [1], replicated, may hold values from 0 to 2016
- noise_bank: float32 [64, 16], replicated, may hold values from -5 to 5
- cond_weight: float32 [16, 256], replicated, may hold values from -1.5 to 1.5
- conv_in: bfloat16 [3, 3, 32, 128], replicated, may hold values from -0.375 to 0.375
- conv_mid: bfloat16 [3, 3, 128, 128], replicated, may hold values from -0.1875 to 0.1875
- conv_out: bfloat16 [3, 3, 128, 128], replicated, may hold values from -0.1875 to 0.1875
- head_weight: bfloat16 [128, 32], replicated, may hold values from -0.5 to 0.5
- per_quantity_offset: float32 [32], replicated, may hold values from -3 to 3
Outputs:
- crps_map: float32 [32, 32, 256], P('tile', 'member')
- conv_grad: float32 [3, 3, 128, 128], replicated
- head_grad: float32 [128, 32], replicated
- bias_grad: float32 [32], replicated
The draws below stay inside these ranges and needn't reach their ends.
Inputs may be any that keep to these rules, and one draw needn't show every extreme that they name: `band_row`: the band lies inside the grid.
All inputs are finite; a program needn't handle non-finite values.
Results may differ from the reference program's by a relative error of at most 0.0015.
Values may be sent and summed in bfloat16 or wider, within the bound.
A program may use at most 64 MiB of HBM per device.

```python
import math
import jax
import jax.numpy as jnp
from jax import lax

VARS = 32
CHANNELS = 128
NOISE = 16
NBANK = 64
GRID_ROWS = 2048
COLS = 256
MEMBERS = 8
ROWS = 32


def plant(drawn, stream_key, least, top_value):
    longest = drawn.shape.index(max(drawn.shape))
    spots = []
    for shift in (0, 1):
        where = [jax.random.randint(jax.random.fold_in(stream_key, axis), (), 0, length) for axis, length in enumerate(drawn.shape)]
        where[longest] = (where[longest] + shift) % drawn.shape[longest]
        spots.append(tuple(where))
    return drawn.at[spots[0]].set(least).at[spots[1]].set(top_value)


def block_scale(key, dims, pieces, least, largest):
    def one(position, parts):
        steps = jax.random.uniform(jax.random.fold_in(jax.random.fold_in(key, 6), position), (parts,), jnp.float32, least / len(pieces), largest / len(pieces))
        return jnp.repeat(jnp.exp(steps), dims[position] // parts).reshape((-1,) + (1,) * (len(dims) - position - 1))

    level = one(*pieces[0])
    for cut in pieces[1:]:
        level = level * one(*cut)
    return level


def bell_draw(own_key, dims, width, bound, shards=(), kind=jnp.bfloat16):
    entries = jax.random.normal(own_key, dims, jnp.float32) * width
    if len(shards) > 0:
        entries = block_scale(own_key, dims, shards, -0.22, 0.18) * entries
    return jnp.clip(entries, min=-bound, max=bound).astype(kind)


def setup_inputs(seed: int = 0) -> dict:
    key_list = jax.random.split(jax.random.key(seed), 12)
    upsampled_coarse = bell_draw(key_list[0], (ROWS, VARS, COLS), 1.0, 6.0, ((0, 8),))
    target = bell_draw(key_list[1], (ROWS, VARS, COLS), 1.0, 6.0, ((0, 8),))
    seeds = plant(jax.random.randint(key_list[2], (MEMBERS,), 0, NBANK), jax.random.fold_in(key_list[2], 1), 0, NBANK - 1).astype(jnp.int32)
    band_row = jax.random.randint(key_list[3], (1,), 0, GRID_ROWS - ROWS + 1).astype(jnp.int32)
    noise_bank = bell_draw(key_list[4], (NBANK, NOISE), 1.0, 5.0, (), jnp.float32)
    cond_weight = bell_draw(key_list[5], (NOISE, 2 * CHANNELS), NOISE ** -0.5, 1.5, (), jnp.float32)
    conv_in = bell_draw(key_list[6], (3, 3, VARS, CHANNELS), (9 * VARS) ** -0.5, 0.375)
    conv_mid = bell_draw(key_list[7], (3, 3, CHANNELS, CHANNELS), (9 * CHANNELS) ** -0.5, 0.1875)
    conv_out = bell_draw(key_list[8], (3, 3, CHANNELS, CHANNELS), (9 * CHANNELS) ** -0.5, 0.1875)
    head_weight = bell_draw(key_list[9], (CHANNELS, VARS), CHANNELS ** -0.5, 0.5)
    per_quantity_offset = bell_draw(key_list[10], (VARS,), 0.5, 3.0, (), jnp.float32)
    return dict(upsampled_coarse=upsampled_coarse, target=target, seeds=seeds, band_row=band_row, noise_bank=noise_bank, cond_weight=cond_weight, conv_in=conv_in, conv_mid=conv_mid, conv_out=conv_out, head_weight=head_weight, per_quantity_offset=per_quantity_offset)


def conv_three(field, kernel):
    row_count = field.shape[0]
    col_count = field.shape[1]
    padded = jnp.pad(field, ((1, 1), (1, 1), (0, 0))).astype(jnp.float32)
    kernel_wide = kernel.astype(jnp.float32)
    summed = jnp.zeros((row_count, col_count, kernel.shape[3]), jnp.float32)
    for i in range(3):
        for j in range(3):
            summed = summed + jnp.einsum('rwc,cd->rwd', padded[i:i + row_count, j:j + col_count], kernel_wide[i, j])
    return summed

def condition(base, cond_scale, cond_shift):
    average = lax.optimization_barrier(jnp.mean(base, axis=-1, keepdims=True))
    centred = base - average
    spread = lax.optimization_barrier(jnp.mean(centred * centred, axis=-1, keepdims=True))
    normed = centred * lax.rsqrt(spread + 1e-05)
    return jax.nn.gelu(normed * (1.0 + cond_scale) + cond_shift).astype(jnp.bfloat16)

def reference(upsampled_coarse, target, seeds, band_row, noise_bank, cond_weight, conv_in, conv_mid, conv_out, head_weight, per_quantity_offset):
    channels = conv_mid.shape[3]
    base = conv_three(jnp.transpose(upsampled_coarse, (0, 2, 1)), conv_in)
    noise_vec = noise_bank[seeds]
    random_latent_gain = jnp.dot(noise_vec, cond_weight, precision=lax.Precision.HIGHEST)

    def evaluate_sample_network(perturbation_line):
        first_hidden = condition(base, perturbation_line[:channels], perturbation_line[channels:])
        latent_layer_two = jax.nn.gelu(conv_three(first_hidden, conv_mid)).astype(jnp.bfloat16)
        final_linear_response = conv_three(latent_layer_two, conv_out)
        latent_layer_three = (first_hidden.astype(jnp.float32) + jax.nn.gelu(final_linear_response)).astype(jnp.bfloat16)
        final_layer_result = jnp.einsum('rwc,cv->rvw', latent_layer_three.astype(jnp.float32), head_weight.astype(jnp.float32))
        sample_prediction = (upsampled_coarse.astype(jnp.float32) + final_layer_result + per_quantity_offset[None, :, None]).astype(jnp.bfloat16)
        return (latent_layer_two, final_linear_response, latent_layer_three, sample_prediction)
    predicted_fields_list = lax.map(lambda perturbation_line: evaluate_sample_network(perturbation_line)[3], random_latent_gain)
    sample_group_predictions = predicted_fields_list.astype(jnp.float32)
    truth = target.astype(jnp.float32)
    member_count = sample_group_predictions.shape[0]

    def pair_terms(member_index):
        differ = member_index[None] - sample_group_predictions
        return (lax.optimization_barrier(jnp.sum(jnp.abs(differ), axis=0)), lax.optimization_barrier(jnp.sum(jnp.sign(differ), axis=0)))
    abs_sums, sign_sums = lax.map(pair_terms, sample_group_predictions)
    crps_map = lax.optimization_barrier(jnp.mean(jnp.abs(sample_group_predictions - truth[None]), axis=0)) - lax.optimization_barrier(jnp.sum(abs_sums, axis=0)) / (2 * member_count * (member_count - 1))
    row_global = band_row[0] + jnp.arange(ROWS, dtype=jnp.int32)
    latitude = math.pi * (row_global.astype(jnp.float32) + 0.5) / GRID_ROWS - math.pi / 2
    row_factor = jnp.cos(latitude) / (ROWS * COLS)
    cotangent = (row_factor[None, :, None, None] * (jnp.sign(sample_group_predictions - truth[None]) / member_count - sign_sums / (member_count * (member_count - 1)))).astype(jnp.bfloat16)

    def member_grads(pair_in):
        perturbation_line, cot_member = pair_in
        latent_layer_two, final_linear_response, latent_layer_three, unused = evaluate_sample_network(perturbation_line)
        cot_wide = cot_member.astype(jnp.float32)
        head_part = jnp.einsum('rwc,rvw->cv', latent_layer_three.astype(jnp.float32), cot_wide)
        bias_part = lax.optimization_barrier(jnp.sum(cot_wide, axis=(0, 2)))
        back = jnp.einsum('rvw,cv->rwc', cot_wide, head_weight.astype(jnp.float32))
        unused_out, pullback = jax.vjp(jax.nn.gelu, final_linear_response)
        d_pre = pullback(back)[0].astype(jnp.bfloat16).astype(jnp.float32)
        padded = jnp.pad(latent_layer_two, ((1, 1), (1, 1), (0, 0))).astype(jnp.float32)
        row_count = d_pre.shape[0]
        col_count = d_pre.shape[1]
        rows_of = []
        for i in range(3):
            cols_of = []
            for j in range(3):
                cols_of.append(jnp.einsum('rwc,rwd->cd', padded[i:i + row_count, j:j + col_count], d_pre))
            rows_of.append(jnp.stack(cols_of))
        return (jnp.stack(rows_of), head_part, bias_part)
    conv_parts, head_parts, bias_parts = lax.map(member_grads, (random_latent_gain, cotangent))
    return (crps_map, lax.optimization_barrier(jnp.sum(conv_parts, axis=0)), lax.optimization_barrier(jnp.sum(head_parts, axis=0)), lax.optimization_barrier(jnp.sum(bias_parts, axis=0)))
```

```python
import functools
import math

import jax
import jax.numpy as jnp
from jax import lax
from jax.experimental import pallas as pl
from jax.experimental.pallas import tpu as pltpu
from jax.sharding import PartitionSpec as P

GRID_ROWS = 2048
HALO = 3
GELU_A = math.sqrt(2.0 / math.pi)
GELU_B = 0.044715
F32 = jnp.float32
BF16 = jnp.bfloat16


def dot(a, b, ca, cb):
    return lax.dot_general(a, b, (((ca,), (cb,)), ((), ())), preferred_element_type=F32)


def gelu(x):
    t = jnp.tanh(GELU_A * (x + GELU_B * (x * x * x)))
    return 0.5 * x * (1.0 + t)


def gelu_and_slope(x):
    sq = x * x
    t = jnp.tanh(GELU_A * (x + GELU_B * (x * sq)))
    half = 0.5 * (1.0 + t)
    slope = half + (0.5 * x) * (1.0 - t * t) * (GELU_A * (1.0 + (3.0 * GELU_B) * sq))
    return x * half, slope


def sign(d):
    return jnp.where(d > 0.0, 1.0, jnp.where(d < 0.0, -1.0, 0.0))


def kernel(
    sizes,
    coarse, target, seeds, band, bank, cond, kin, kmid, kout, head, offset,
    crps, cgrad, hgrad, bgrad,
    xin, kcat, headt, s1, s2, third, slope, dpre, fc, cot, rfac, score,
    acc, rc, rx, rt, total,
    halo_send, halo_recv, fc_send, fc_recv,
    c_send, c_recv, x_send, x_recv, t_send, t_recv,
    gt_send, gt_recv, gx_send, gx_recv, gc_send, gc_recv,
):
    M, T, mm, R, V, W, C, N = sizes
    me = lax.axis_index("member")
    tile = lax.axis_index("tile")
    X = M // 2
    core = lax.rem(me, 2)
    xi = me // 2
    members = M * mm

    def remote(src, dst, ss, rs, member, tl):
        return pltpu.make_async_remote_copy(
            src_ref=src, dst_ref=dst, send_sem=ss, recv_sem=rs,
            device_id=(member, tl), device_id_type=pl.DeviceIdType.MESH,
        )

    barrier = pltpu.get_barrier_semaphore()
    for d in range(1, M):
        pl.semaphore_signal(barrier, inc=1, device_id=(lax.rem(me + d, M), tile),
                            device_id_type=pl.DeviceIdType.MESH)
    for d in range(1, T):
        pl.semaphore_signal(barrier, inc=1, device_id=(me, lax.rem(tile + d, T)),
                            device_id_type=pl.DeviceIdType.MESH)

    xin[HALO:HALO + R] = coarse[...]
    for i in range(3):
        for j in range(3):
            kcat[V * i:V * (i + 1), C * j:C * (j + 1)] = kin[3 * i + j]
    headt[...] = head[...].astype(F32).T.astype(BF16)
    noise = jnp.concatenate([bank[pl.ds(seeds[m], 1), :] for m in range(mm)], axis=0)
    latent = jnp.dot(noise, cond[...], precision=lax.Precision.HIGHEST,
                     preferred_element_type=F32)
    rows8 = rfac.shape[0]
    row = lax.broadcasted_iota(jnp.int32, (rows8, 128), 0) + (band[0] + tile * R)
    lat = math.pi * (row.astype(F32) + 0.5) / GRID_ROWS - math.pi / 2
    rfac[...] = jnp.cos(lat) / (T * R * W)
    eye = lax.broadcasted_iota(jnp.int32, (V, V), 0) == lax.broadcasted_iota(jnp.int32, (V, V), 1)
    off_col = jnp.sum(jnp.where(eye, jnp.broadcast_to(offset[...], (V, V)), 0.0), axis=1,
                      keepdims=True)
    acc[9 * C:N, :] = jnp.zeros((N - 9 * C, 128), F32)

    pl.semaphore_wait(barrier, (M - 1) + (T - 1))

    down = remote(xin.at[R:R + HALO], xin.at[0:HALO], halo_send.at[0], halo_recv.at[0],
                  me, lax.rem(tile + 1, T))
    up = remote(xin.at[HALO:2 * HALO], xin.at[HALO + R:2 * HALO + R], halo_send.at[1],
                halo_recv.at[1], me, lax.rem(tile + T - 1, T))

    @pl.when(tile < T - 1)
    def _():
        down.start()

    @pl.when(tile > 0)
    def _():
        up.start()

    @pl.when(tile > 0)
    def _():
        down.wait_recv()

    @pl.when(tile < T - 1)
    def _():
        up.wait_recv()

    @pl.when(tile == 0)
    def _():
        xin[0:HALO] = jnp.zeros((HALO, V, W), BF16)

    @pl.when(tile == T - 1)
    def _():
        xin[HALO + R:2 * HALO + R] = jnp.zeros((HALO, V, W), BF16)

    def shift_down(x):
        w = lax.broadcasted_iota(jnp.int32, x.shape, 0)
        return jnp.where(w == 0, 0.0, pltpu.roll(x, 1, 0))

    def shift_up(x):
        w = lax.broadcasted_iota(jnp.int32, x.shape, 0)
        return jnp.where(w == W - 1, 0.0, pltpu.roll(x, W - 1, 0))

    def put_shifted(dst, m, q, x):
        dst[m, q, :, 0:C] = shift_down(x).astype(BF16)
        dst[m, q, :, C:2 * C] = x.astype(BF16)
        dst[m, q, :, 2 * C:3 * C] = shift_up(x).astype(BF16)

    def inside(grow):
        return jnp.logical_and(grow >= 0, grow < T * R)

    def first_row(q, carry):
        p = dot(xin[pl.ds(q, 3)].reshape(3 * V, W), kcat[...], 0, 0)
        base = shift_down(p[:, 0:C]) + p[:, C:2 * C] + shift_up(p[:, 2 * C:3 * C])
        centred = base - jnp.mean(base, axis=-1, keepdims=True)
        spread = jnp.mean(centred * centred, axis=-1, keepdims=True)
        normed = centred * lax.rsqrt(spread + 1e-05)
        ok = inside(tile * R + q - 2)
        for m in range(mm):
            mixed = normed * (1.0 + latent[m:m + 1, 0:C]) + latent[m:m + 1, C:2 * C]
            put_shifted(s1, m, q, jnp.where(ok, gelu(mixed), 0.0))
        return carry

    lax.fori_loop(0, R + 4, first_row, 0)

    def fc_copy(m, d, slot):
        return remote(fc.at[slot], fc.at[slot], fc_send.at[m, d - 1], fc_recv.at[m, d - 1],
                      lax.rem(me + d, M), tile)

    for m in range(mm):
        def second_row(q, carry, m=m):
            h = dot(s1[m, q], kmid[0], 1, 0)
            h = h + dot(s1[m, q + 1], kmid[1], 1, 0)
            h = h + dot(s1[m, q + 2], kmid[2], 1, 0)
            put_shifted(s2, m, q, jnp.where(inside(tile * R + q - 1), gelu(h), 0.0))
            return carry

        lax.fori_loop(0, R + 2, second_row, 0)
        slot = me * mm + m

        def out_row(r, carry, m=m, slot=slot):
            h = dot(s2[m, r], kout[0], 1, 0)
            h = h + dot(s2[m, r + 1], kout[1], 1, 0)
            h = h + dot(s2[m, r + 2], kout[2], 1, 0)
            g, s = gelu_and_slope(h)
            slope[m, r] = s
            feat = (s1[m, r + 2, :, C:2 * C].astype(F32) + g).astype(BF16)
            third[m, r] = feat
            f = dot(headt[...], feat, 1, 1) + coarse[r].astype(F32) + off_col
            fc[slot, r] = f.astype(BF16)
            return carry

        lax.fori_loop(0, R, out_row, 0)
        for d in range(1, M):
            fc_copy(m, d, slot).start()

    for m in range(mm):
        for d in range(1, M):
            fc_copy(m, d, lax.rem(me + M - d, M) * mm + m).wait_recv()

    def cot_row(r, carry):
        truth = target[r].astype(F32)
        factor = rfac[pl.ds(r, 1), 0:1]
        for m in range(mm):
            f = fc[me * mm + m, r].astype(F32)
            s = jnp.zeros_like(f)
            for j in range(members):
                s = s + sign(f - fc[j, r].astype(F32))
            c = factor * (sign(f - truth) / members - s / (members * (members - 1)))
            cb = c.astype(BF16)
            cot[m, r] = cb
            back = dot(cb, headt[...], 0, 0)
            dpre[m, r] = (back * slope[m, r]).astype(BF16)
            acc[9 * C:9 * C + V, :] += dot(cb, third[m, r], 1, 0)
            acc[9 * C + V:9 * C + V + 8, 0:V] += dot(jnp.ones((8, W), BF16), cb, 1, 1)
        return carry

    lax.fori_loop(0, R, cot_row, 0)

    for i in range(3):
        g = jnp.zeros((3 * C, C), F32)
        for m in range(mm):
            g = g + dot(s2[m, i:i + R].reshape(R * W, 3 * C), dpre[m].reshape(R * W, C), 0, 0)
        acc[3 * C * i:3 * C * (i + 1), :] = g

    half, chunk, piece = N // 2, N // M, N // (M * T)
    mate = me + 1 - 2 * core
    my_half = pl.multiple_of(core * half, 8)
    other_half = pl.multiple_of((1 - core) * half, 8)
    cc = remote(acc.at[pl.ds(other_half, half)], rc, c_send, c_recv, mate, tile)
    cc.start()

    def crps_row(r, carry):
        truth = target[r].astype(F32)
        fs = [fc[j, r].astype(F32) for j in range(members)]
        near = jnp.zeros_like(truth)
        pair = jnp.zeros_like(truth)
        for i in range(members):
            near = near + jnp.abs(fs[i] - truth)
            for j in range(i + 1, members):
                pair = pair + jnp.abs(fs[i] - fs[j])
        score[r] = near / members - (2.0 * pair) / (2 * members * (members - 1))
        return carry

    lax.fori_loop(0, R, crps_row, 0)
    share = V // M
    for k in range(M):
        @pl.when(me == k)
        def _(k=k):
            crps[...] = score[:, share * k:share * (k + 1), :]

    cc.wait_recv()
    acc[pl.ds(my_half, half), :] += rc[...]

    def x_at(x):
        return pl.multiple_of(core * half + x * chunk, 8)

    xs = []
    for d in range(1, X):
        to = lax.rem(xi + d, X)
        xs.append(remote(acc.at[pl.ds(x_at(to), chunk)], rx.at[d - 1], x_send.at[d - 1],
                         x_recv.at[d - 1], to * 2 + core, tile))
    for cp in xs:
        cp.start()
    for d in range(1, X):
        xs[d - 1].wait_recv()
        acc[pl.ds(x_at(xi), chunk), :] += rx[d - 1]

    def t_at(x, t):
        return pl.multiple_of(core * half + x * chunk + t * piece, 8)

    ts = []
    for d in range(1, T):
        to = lax.rem(tile + d, T)
        ts.append(remote(acc.at[pl.ds(t_at(xi, to), piece)], rt.at[d - 1], t_send.at[d - 1],
                         t_recv.at[d - 1], me, to))
    for cp in ts:
        cp.start()
    own = acc[pl.ds(t_at(xi, tile), piece), :]
    for d in range(1, T):
        ts[d - 1].wait_recv()
        own = own + rt[d - 1]
    total[pl.ds(t_at(xi, tile), piece), :] = own

    def here(x, t):
        return total.at[pl.ds(t_at(x, t), piece)]

    def gt_copy(d, t):
        return remote(here(xi, t), here(xi, t), gt_send.at[d - 1], gt_recv.at[d - 1],
                      me, lax.rem(tile + d, T))

    def gx_copy(d, k, x, t):
        return remote(here(x, t), here(x, t), gx_send.at[d - 1, k], gx_recv.at[d - 1, k],
                      lax.rem(xi + d, X) * 2 + core, tile)

    def gc_copy(d, k, x, t, c):
        at = pl.multiple_of(c * half + x * chunk + t * piece, 8)
        ref = total.at[pl.ds(at, piece)]
        return remote(ref, ref, gc_send.at[d, k], gc_recv.at[d, k], mate, tile)

    for d in range(1, T):
        gt_copy(d, tile).start()
    for k in range(T):
        t = lax.rem(tile + T - k, T)
        if k > 0:
            gt_copy(k, t).wait_recv()
        for d in range(1, X):
            gx_copy(d, k, xi, t).start()
        gc_copy(0, k, xi, t, core).start()
    for k in range(T):
        t = lax.rem(tile + T - k, T)
        for d in range(1, X):
            x = lax.rem(xi + X - d, X)
            gx_copy(d, k, x, t).wait_recv()
            gc_copy(d, k, x, t, core).start()
    for k in range(T):
        t = lax.rem(tile + T - k, T)
        for d in range(X):
            gc_copy(d, k, lax.rem(xi + X - d, X), t, 1 - core).wait_recv()

    cgrad[...] = total[0:9 * C, :]
    hgrad[...] = total[9 * C:9 * C + V, :].T
    bgrad[...] = total[9 * C + V:9 * C + V + 1, 0:V]

    @pl.when(tile < T - 1)
    def _():
        down.wait_send()

    @pl.when(tile > 0)
    def _():
        up.wait_send()

    for m in range(mm):
        for d in range(1, M):
            fc_copy(m, d, me * mm + m).wait_send()
    cc.wait_send()
    for cp in xs + ts:
        cp.wait_send()
    for d in range(1, T):
        gt_copy(d, tile).wait_send()
    for k in range(T):
        t = lax.rem(tile + T - k, T)
        for d in range(1, X):
            gx_copy(d, k, xi, t).wait_send()
        for d in range(X):
            gc_copy(d, k, lax.rem(xi + X - d, X), t, core).wait_send()


def on_device(coarse, target, seeds, band, bank, cond, kin, kmid, kout, head, offset):
    M, T = lax.axis_size("member"), lax.axis_size("tile")
    mm = seeds.shape[0]
    R, V, W = coarse.shape
    C = kmid.shape[3]
    unit = 8 * M * T
    N = -(-(9 * C + V + 8) // unit) * unit
    X = M // 2
    sizes = (M, T, mm, R, V, W, C, N)
    vmem = pl.BlockSpec(memory_space=pltpu.VMEM)
    smem = pl.BlockSpec(memory_space=pltpu.SMEM)
    dma = pltpu.SemaphoreType.DMA
    scratch = [
        pltpu.VMEM((R + 2 * HALO, V, W), BF16),
        pltpu.VMEM((3 * V, 3 * C), BF16),
        pltpu.VMEM((V, C), BF16),
        pltpu.VMEM((mm, R + 4, W, 3 * C), BF16),
        pltpu.VMEM((mm, R + 2, W, 3 * C), BF16),
        pltpu.VMEM((mm, R, W, C), BF16),
        pltpu.VMEM((mm, R, W, C), F32),
        pltpu.VMEM((mm, R, W, C), BF16),
        pltpu.VMEM((M * mm, R, V, W), BF16),
        pltpu.VMEM((mm, R, V, W), BF16),
        pltpu.VMEM((-(-R // 8) * 8, 128), F32),
        pltpu.VMEM((R, V, W), F32),
        pltpu.VMEM((N, C), F32),
        pltpu.VMEM((N // 2, C), F32),
        pltpu.VMEM((max(X - 1, 1), N // M, C), F32),
        pltpu.VMEM((T - 1, N // (M * T), C), F32),
        pltpu.VMEM((N, C), F32),
        dma((2,)), dma((2,)), dma((mm, M - 1)), dma((mm, M - 1)),
        dma, dma, dma((max(X - 1, 1),)), dma((max(X - 1, 1),)), dma((T - 1,)), dma((T - 1,)),
        dma((T - 1,)), dma((T - 1,)), dma((max(X - 1, 1), T)), dma((max(X - 1, 1), T)),
        dma((X, T)), dma((X, T)),
    ]
    crps, cgrad, hgrad, bgrad = pl.pallas_call(
        functools.partial(kernel, sizes),
        out_shape=(
            jax.ShapeDtypeStruct((R, V // M, W), F32),
            jax.ShapeDtypeStruct((9 * C, C), F32),
            jax.ShapeDtypeStruct((C, V), F32),
            jax.ShapeDtypeStruct((1, V), F32),
        ),
        in_specs=[vmem, vmem, smem, smem] + [vmem] * 7,
        out_specs=(vmem,) * 4,
        scratch_shapes=scratch,
        compiler_params=pltpu.CompilerParams(
            collective_id=0, has_side_effects=True, vmem_limit_bytes=48 * 1024 * 1024
        ),
    )(
        coarse, target, seeds, band, bank, cond,
        kin.reshape(9, V, C), kmid.reshape(3, 3 * C, C), kout.reshape(3, 3 * C, C),
        head, offset.reshape(1, V),
    )
    return crps, cgrad.reshape(3, 3, C, C), hgrad, bgrad.reshape(V)


def solution(mesh):
    return jax.shard_map(
        on_device,
        mesh=mesh,
        in_specs=(P("tile", None, None), P("tile", None, None), P("member")) + (P(),) * 8,
        out_specs=(P("tile", "member", None), P(), P(), P()),
        check_vma=False,
    )
```

```python
import functools
import math

import jax
import jax.numpy as jnp
from jax import lax
from jax.experimental import pallas as pl
from jax.experimental.pallas import tpu as pltpu
from jax.sharding import PartitionSpec as P

GRID_ROWS = 2048
HALO = 3
GELU_A = math.sqrt(2.0 / math.pi)
GELU_B = 0.044715
F32 = jnp.float32
BF16 = jnp.bfloat16


def dot(a, b, ca, cb):
    return lax.dot_general(a, b, (((ca,), (cb,)), ((), ())), preferred_element_type=F32)


def gelu(x):
    t = jnp.tanh(GELU_A * (x + GELU_B * (x * x * x)))
    return 0.5 * x * (1.0 + t)


def gelu_and_slope(x):
    sq = x * x
    t = jnp.tanh(GELU_A * (x + GELU_B * (x * sq)))
    half = 0.5 * (1.0 + t)
    slope = half + (0.5 * x) * (1.0 - t * t) * (GELU_A * (1.0 + (3.0 * GELU_B) * sq))
    return x * half, slope


def sign(d):
    return jnp.where(d > 0.0, 1.0, jnp.where(d < 0.0, -1.0, 0.0))


def kernel(
    sizes,
    seeds, band, coarse_h, kin_h, bank_h, cond_h, offset_h, head_h, kmid_h, kout_h, target_h,
    crps, cgrad, hgrad, bgrad,
    kin, bank, cond, offset, headt, kmid, kout, target, in_sem,
    xin, kcat, s1, s2, third, slope, dpre, fc, cot, rfac, score,
    acc, rc, rx, quarter, rt, total,
    halo_send, halo_recv, fc_send, fc_recv,
    c_send, c_recv, x_send, x_recv, t_send, t_recv,
    gt_send, gt_recv, gx_send, gx_recv, gc_send, gc_recv,
):
    M, T, mm, R, V, W, C, E, per = sizes
    me = lax.axis_index("member")
    tile = lax.axis_index("tile")
    X = M // 2
    core = lax.rem(me, 2)
    xi = me // 2
    members = M * mm

    def remote(src, dst, ss, rs, member, tl):
        return pltpu.make_async_remote_copy(
            src_ref=src, dst_ref=dst, send_sem=ss, recv_sem=rs,
            device_id=(member, tl), device_id_type=pl.DeviceIdType.MESH,
        )

    barrier = pltpu.get_barrier_semaphore()
    for d in range(1, M):
        pl.semaphore_signal(barrier, inc=1, device_id=(lax.rem(me + d, M), tile),
                            device_id_type=pl.DeviceIdType.MESH)
    for d in range(1, T):
        pl.semaphore_signal(barrier, inc=1, device_id=(me, lax.rem(tile + d, T)),
                            device_id_type=pl.DeviceIdType.MESH)

    loads = [
        pltpu.make_async_copy(src, dst, in_sem.at[k])
        for k, (src, dst) in enumerate([
            (coarse_h, xin.at[HALO:HALO + R]), (kin_h, kin), (bank_h, bank), (cond_h, cond),
            (offset_h, offset), (head_h, headt), (kmid_h, kmid), (kout_h, kout),
            (target_h, target),
        ])
    ]
    for cp in loads:
        cp.start()

    for cp in loads[1:6]:
        cp.wait()
    for i in range(3):
        for j in range(3):
            kcat[V * i:V * (i + 1), C * j:C * (j + 1)] = kin[3 * i + j]
    lane = lax.broadcasted_iota(jnp.int32, bank.shape, 1)
    latent = []
    for m in range(mm):
        noise = jnp.sum(jnp.where(lane == seeds[m], bank[...], 0.0), axis=1, keepdims=True)
        latent.append(jnp.sum(noise * cond[...], axis=0, keepdims=True))
    rows8 = rfac.shape[0]
    row = lax.broadcasted_iota(jnp.int32, (rows8, 128), 0) + (band[0] + tile * R)
    lat = math.pi * (row.astype(F32) + 0.5) / GRID_ROWS - math.pi / 2
    rfac[...] = jnp.cos(lat) / (T * R * W)
    eye = lax.broadcasted_iota(jnp.int32, (V, V), 0) == lax.broadcasted_iota(jnp.int32, (V, V), 1)
    off_col = jnp.sum(jnp.where(eye, jnp.broadcast_to(offset[...], (V, V)), 0.0), axis=1,
                      keepdims=True)
    acc[0:E, :] = jnp.zeros((E, C), F32)

    pl.semaphore_wait(barrier, (M - 1) + (T - 1))

    down = remote(coarse_h.at[R - HALO:R], xin.at[0:HALO], halo_send.at[0], halo_recv.at[0],
                  me, lax.rem(tile + 1, T))
    up = remote(coarse_h.at[0:HALO], xin.at[HALO + R:2 * HALO + R], halo_send.at[1],
                halo_recv.at[1], me, lax.rem(tile + T - 1, T))

    @pl.when(tile < T - 1)
    def _():
        down.start()

    @pl.when(tile > 0)
    def _():
        up.start()

    loads[0].wait()

    @pl.when(tile > 0)
    def _():
        down.wait_recv()

    @pl.when(tile < T - 1)
    def _():
        up.wait_recv()

    @pl.when(tile == 0)
    def _():
        xin[0:HALO] = jnp.zeros((HALO, V, W), BF16)

    @pl.when(tile == T - 1)
    def _():
        xin[HALO + R:2 * HALO + R] = jnp.zeros((HALO, V, W), BF16)

    def shift_down(x):
        w = lax.broadcasted_iota(jnp.int32, x.shape, 0)
        return jnp.where(w == 0, 0.0, pltpu.roll(x, 1, 0))

    def shift_up(x):
        w = lax.broadcasted_iota(jnp.int32, x.shape, 0)
        return jnp.where(w == W - 1, 0.0, pltpu.roll(x, W - 1, 0))

    def put_shifted(dst, m, q, x):
        dst[m, q, :, 0:C] = shift_down(x).astype(BF16)
        dst[m, q, :, C:2 * C] = x.astype(BF16)
        dst[m, q, :, 2 * C:3 * C] = shift_up(x).astype(BF16)

    def inside(grow):
        return jnp.logical_and(grow >= 0, grow < T * R)

    def rows(count, body):
        step = 2 if count % 2 == 0 else 1

        def several(q, carry):
            for k in range(step):
                body(q * step + k, carry)
            return carry

        lax.fori_loop(0, count // step, several, 0)

    def first_row(q, carry):
        p = dot(xin[pl.ds(q, 3)].reshape(3 * V, W), kcat[...], 0, 0)
        base = shift_down(p[:, 0:C]) + p[:, C:2 * C] + shift_up(p[:, 2 * C:3 * C])
        centred = base - jnp.mean(base, axis=-1, keepdims=True)
        spread = jnp.mean(centred * centred, axis=-1, keepdims=True)
        normed = centred * lax.rsqrt(spread + 1e-05)
        ok = inside(tile * R + q - 2)
        for m in range(mm):
            mixed = normed * (1.0 + latent[m][:, 0:C]) + latent[m][:, C:2 * C]
            put_shifted(s1, m, q, jnp.where(ok, gelu(mixed), 0.0))
        return carry

    rows(R + 4, first_row)
    loads[6].wait()
    loads[7].wait()

    def fc_copy(m, d, slot):
        return remote(fc.at[slot], fc.at[slot], fc_send.at[m, d - 1], fc_recv.at[m, d - 1],
                      lax.rem(me + d, M), tile)

    for m in range(mm):
        def second_row(q, carry, m=m):
            h = dot(s1[m, q], kmid[0], 1, 0)
            h = h + dot(s1[m, q + 1], kmid[1], 1, 0)
            h = h + dot(s1[m, q + 2], kmid[2], 1, 0)
            put_shifted(s2, m, q, jnp.where(inside(tile * R + q - 1), gelu(h), 0.0))
            return carry

        rows(R + 2, second_row)
        slot = me * mm + m

        def out_row(r, carry, m=m, slot=slot):
            h = dot(s2[m, r], kout[0], 1, 0)
            h = h + dot(s2[m, r + 1], kout[1], 1, 0)
            h = h + dot(s2[m, r + 2], kout[2], 1, 0)
            g, s = gelu_and_slope(h)
            slope[m, r] = s
            feat = (s1[m, r + 2, :, C:2 * C].astype(F32) + g).astype(BF16)
            third[m, r] = feat
            f = dot(headt[...], feat, 1, 1) + xin[HALO + r].astype(F32) + off_col
            fc[slot, r] = f.astype(BF16)
            return carry

        rows(R, out_row)
        for d in range(1, M):
            fc_copy(m, d, slot).start()

    loads[8].wait()
    for m in range(mm):
        for d in range(1, M):
            fc_copy(m, d, lax.rem(me + M - d, M) * mm + m).wait_recv()

    def cot_row(r, carry):
        truth = target[r].astype(F32)
        factor = rfac[pl.ds(r, 1), 0:1]
        for m in range(mm):
            f = fc[me * mm + m, r].astype(F32)
            s = jnp.zeros_like(f)
            for j in range(members):
                s = s + sign(f - fc[j, r].astype(F32))
            c = factor * (sign(f - truth) / members - s / (members * (members - 1)))
            cb = c.astype(BF16)
            cot[m, r] = cb
            back = dot(cb, headt[...], 0, 0)
            dpre[m, r] = (back * slope[m, r]).astype(BF16)
            acc[0:V, :] += dot(cb, third[m, r], 1, 0)
            acc[V:V + 8, 0:V] += dot(jnp.ones((8, W), BF16), cb, 1, 1)
        return carry

    rows(R, cot_row)

    mate = me + 1 - 2 * core
    sizes_b = (E, 3 * C, 3 * C, 3 * C)

    def mine(b, c, x, part):
        first = sum(sizes_b[:b]) + c * (sizes_b[b] // 2) + x * (sizes_b[b] // M)
        return pl.ds(pl.multiple_of(first, 8), part)

    def c_copy(b):
        h = sizes_b[b] // 2
        at = sum(sizes_b[:b]) // 2
        return remote(acc.at[mine(b, 1 - core, 0, h)], rc.at[at:at + h], c_send.at[b],
                      c_recv.at[b], mate, tile)

    def x_copy(b, d):
        part = sizes_b[b] // M
        at = sum(sizes_b[:b]) // M
        to = lax.rem(xi + d, X)
        return remote(acc.at[mine(b, core, to, part)], rx.at[d - 1, at:at + part],
                      x_send.at[d - 1, b], x_recv.at[d - 1, b], to * 2 + core, tile)

    def core_sum(b):
        h = sizes_b[b] // 2
        at = sum(sizes_b[:b]) // 2
        c_copy(b).wait_recv()
        acc[mine(b, core, 0, h), :] += rc[at:at + h]
        for d in range(1, X):
            x_copy(b, d).start()

    def chunk_sum(b):
        part = sizes_b[b] // M
        at = sum(sizes_b[:b]) // M
        own = acc[mine(b, core, xi, part), :]
        for d in range(1, X):
            x_copy(b, d).wait_recv()
            own = own + rx[d - 1, at:at + part]
        quarter[at:at + part, :] = own

    c_copy(0).start()
    for i in range(3):
        g = jnp.zeros((3 * C, C), F32)
        for m in range(mm):
            g = g + dot(s2[m, i:i + R].reshape(R * W, 3 * C), dpre[m].reshape(R * W, C), 0, 0)
        acc[E + 3 * C * i:E + 3 * C * (i + 1), :] = g
        c_copy(i + 1).start()
        core_sum(i)

    def crps_row(r, carry):
        truth = target[r].astype(F32)
        fs = [fc[j, r].astype(F32) for j in range(members)]
        near = jnp.zeros_like(truth)
        pair = jnp.zeros_like(truth)
        for i in range(members):
            near = near + jnp.abs(fs[i] - truth)
            for j in range(i + 1, members):
                pair = pair + jnp.abs(fs[i] - fs[j])
        score[r] = near / members - (2.0 * pair) / (2 * members * (members - 1))
        return carry

    core_sum(3)
    rows(R, crps_row)
    share = V // M
    for k in range(M):
        @pl.when(me == k)
        def _(k=k):
            crps[...] = score[:, share * k:share * (k + 1), :]

    for b in range(4):
        chunk_sum(b)

    half, chunk, piece = X * per, per, per // T

    def t_at(x, t):
        return pl.multiple_of(core * half + x * chunk + t * piece, 8)

    ts = []
    for d in range(1, T):
        to = lax.rem(tile + d, T)
        ts.append(remote(quarter.at[pl.ds(pl.multiple_of(to * piece, 8), piece)], rt.at[d - 1], t_send.at[d - 1],
                         t_recv.at[d - 1], me, to))
    for cp in ts:
        cp.start()
    own = quarter[pl.ds(pl.multiple_of(tile * piece, 8), piece), :]
    for d in range(1, T):
        ts[d - 1].wait_recv()
        own = own + rt[d - 1]
    total[pl.ds(t_at(xi, tile), piece), :] = own

    def here(x, t):
        return total.at[pl.ds(t_at(x, t), piece)]

    def gt_copy(d, t):
        return remote(here(xi, t), here(xi, t), gt_send.at[d - 1], gt_recv.at[d - 1],
                      me, lax.rem(tile + d, T))

    def gx_copy(d, k, x, t):
        return remote(here(x, t), here(x, t), gx_send.at[d - 1, k], gx_recv.at[d - 1, k],
                      lax.rem(xi + d, X) * 2 + core, tile)

    def gc_copy(d, k, x, t, c):
        at = pl.multiple_of(c * half + x * chunk + t * piece, 8)
        ref = total.at[pl.ds(at, piece)]
        return remote(ref, ref, gc_send.at[d, k], gc_recv.at[d, k], mate, tile)

    for d in range(1, T):
        gt_copy(d, tile).start()
    for k in range(T):
        t = lax.rem(tile + T - k, T)
        if k > 0:
            gt_copy(k, t).wait_recv()
        for d in range(1, X):
            gx_copy(d, k, xi, t).start()
        gc_copy(0, k, xi, t, core).start()
    for k in range(T):
        t = lax.rem(tile + T - k, T)
        for d in range(1, X):
            x = lax.rem(xi + X - d, X)
            gx_copy(d, k, x, t).wait_recv()
            gc_copy(d, k, x, t, core).start()
    for k in range(T):
        t = lax.rem(tile + T - k, T)
        for d in range(X):
            gc_copy(d, k, lax.rem(xi + X - d, X), t, 1 - core).wait_recv()

    extra, part = E // M, 3 * C // M
    for q in range(M):
        for i in range(3):
            at = per * q + extra + part * i
            cgrad[3 * C * i + part * q:3 * C * i + part * (q + 1), :] = total[at:at + part, :]
    hgrad[...] = total[0:V, :]
    at = per * (V // extra) + V % extra
    bgrad[...] = total[at:at + 1, 0:V]

    @pl.when(tile < T - 1)
    def _():
        down.wait_send()

    @pl.when(tile > 0)
    def _():
        up.wait_send()

    for m in range(mm):
        for d in range(1, M):
            fc_copy(m, d, me * mm + m).wait_send()
    for b in range(4):
        c_copy(b).wait_send()
        for d in range(1, X):
            x_copy(b, d).wait_send()
    for cp in ts:
        cp.wait_send()
    for d in range(1, T):
        gt_copy(d, tile).wait_send()
    for k in range(T):
        t = lax.rem(tile + T - k, T)
        for d in range(1, X):
            gx_copy(d, k, xi, t).wait_send()
        for d in range(X):
            gc_copy(d, k, lax.rem(xi + X - d, X), t, core).wait_send()


def on_device(coarse, target, seeds, band, bank, cond, kin, kmid, kout, head, offset):
    M, T = lax.axis_size("member"), lax.axis_size("tile")
    mm = seeds.shape[0]
    R, V, W = coarse.shape
    C = kmid.shape[3]
    extra = -(-V // 8) * 8
    while (9 * C // M + extra) % (8 * T) or extra * M < V + 8:
        extra += 8
    E, per = extra * M, 9 * C // M + extra
    N = per * M
    X = M // 2
    sizes = (M, T, mm, R, V, W, C, E, per)
    vmem = pl.BlockSpec(memory_space=pltpu.VMEM)
    smem = pl.BlockSpec(memory_space=pltpu.SMEM)
    dma = pltpu.SemaphoreType.DMA
    scratch = [
        pltpu.VMEM((9, V, C), BF16),
        pltpu.VMEM(bank.shape[::-1], F32),
        pltpu.VMEM(cond.shape, F32),
        pltpu.VMEM((1, V), F32),
        pltpu.VMEM((V, C), BF16),
        pltpu.VMEM((3, 3 * C, C), BF16),
        pltpu.VMEM((3, 3 * C, C), BF16),
        pltpu.VMEM((R, V, W), BF16),
        dma((9,)),
        pltpu.VMEM((R + 2 * HALO, V, W), BF16),
        pltpu.VMEM((3 * V, 3 * C), BF16),
        pltpu.VMEM((mm, R + 4, W, 3 * C), BF16),
        pltpu.VMEM((mm, R + 2, W, 3 * C), BF16),
        pltpu.VMEM((mm, R, W, C), BF16),
        pltpu.VMEM((mm, R, W, C), F32),
        pltpu.VMEM((mm, R, W, C), BF16),
        pltpu.VMEM((M * mm, R, V, W), BF16),
        pltpu.VMEM((mm, R, V, W), BF16),
        pltpu.VMEM((-(-R // 8) * 8, 128), F32),
        pltpu.VMEM((R, V, W), F32),
        pltpu.VMEM((N, C), F32),
        pltpu.VMEM((N // 2, C), F32),
        pltpu.VMEM((max(X - 1, 1), per, C), F32),
        pltpu.VMEM((per, C), F32),
        pltpu.VMEM((T - 1, N // (M * T), C), F32),
        pltpu.VMEM((N, C), F32),
        dma((2,)), dma((2,)), dma((mm, M - 1)), dma((mm, M - 1)),
        dma((4,)), dma((4,)), dma((max(X - 1, 1), 4)), dma((max(X - 1, 1), 4)), dma((T - 1,)), dma((T - 1,)),
        dma((T - 1,)), dma((T - 1,)), dma((max(X - 1, 1), T)), dma((max(X - 1, 1), T)),
        dma((X, T)), dma((X, T)),
    ]
    crps, cgrad, hgrad, bgrad = pl.pallas_call(
        functools.partial(kernel, sizes),
        out_shape=(
            jax.ShapeDtypeStruct((R, V // M, W), F32),
            jax.ShapeDtypeStruct((9 * C, C), F32),
            jax.ShapeDtypeStruct((V, C), F32),
            jax.ShapeDtypeStruct((1, V), F32),
        ),
        in_specs=[smem, smem] + [pl.BlockSpec(memory_space=pltpu.HBM)] * 9,
        out_specs=(vmem,) * 4,
        scratch_shapes=scratch,
        compiler_params=pltpu.CompilerParams(
            collective_id=0, has_side_effects=True, vmem_limit_bytes=63 * 1024 * 1024
        ),
    )(
        seeds, band, coarse, kin.reshape(9, V, C), bank.T, cond, offset.reshape(1, V), head.T,
        kmid.reshape(3, 3 * C, C), kout.reshape(3, 3 * C, C), target,
    )
    return crps, cgrad.reshape(3, 3, C, C), hgrad.T, bgrad.reshape(V)


def solution(mesh):
    return jax.shard_map(
        on_device,
        mesh=mesh,
        in_specs=(P("tile", None, None), P("tile", None, None), P("member")) + (P(),) * 8,
        out_specs=(P("tile", "member", None), P(), P(), P()),
        check_vma=False,
    )
```

```python
import functools
import math

import jax
import jax.numpy as jnp
from jax import lax
from jax.experimental import pallas as pl
from jax.experimental.pallas import tpu as pltpu
from jax.sharding import PartitionSpec as P

GRID_ROWS = 2048
HALO = 3
GELU_A = math.sqrt(2.0 / math.pi)
GELU_B = 0.044715
F32 = jnp.float32
BF16 = jnp.bfloat16


def dot(a, b, ca, cb):
    return lax.dot_general(a, b, (((ca,), (cb,)), ((), ())), preferred_element_type=F32)


def gelu(x):
    t = jnp.tanh(GELU_A * (x + GELU_B * (x * x * x)))
    return 0.5 * x * (1.0 + t)


def gelu_and_slope(x):
    sq = x * x
    t = jnp.tanh(GELU_A * (x + GELU_B * (x * sq)))
    half = 0.5 * (1.0 + t)
    slope = half + (0.5 * x) * (1.0 - t * t) * (GELU_A * (1.0 + (3.0 * GELU_B) * sq))
    return x * half, slope


def sign(d):
    return jnp.where(d > 0.0, 1.0, jnp.where(d < 0.0, -1.0, 0.0))


def kernel(
    sizes,
    seeds, band, coarse_h, kin_h, bank_h, cond_h, offset_h, head_h, kmid_h, kout_h, target_h,
    crps, cgrad, hgrad, bgrad,
    kin, bank, cond, offset, headt, kmid, kout, target, in_sem,
    xin, kcat, s1, s2, third, slope, dpre, fc, cot, rfac, score,
    acc, rc, rx, quarter, rt, total,
    halo_send, halo_recv, fc_send, fc_recv,
    c_send, c_recv, x_send, x_recv, t_send, t_recv,
    gt_send, gt_recv, gx_send, gx_recv, gc_send, gc_recv,
):
    M, T, mm, R, V, W, C, E, per = sizes
    me = lax.axis_index("member")
    tile = lax.axis_index("tile")
    X = M // 2
    core = lax.rem(me, 2)
    xi = me // 2
    members = M * mm

    def remote(src, dst, ss, rs, member, tl):
        return pltpu.make_async_remote_copy(
            src_ref=src, dst_ref=dst, send_sem=ss, recv_sem=rs,
            device_id=(member, tl), device_id_type=pl.DeviceIdType.MESH,
        )

    barrier = pltpu.get_barrier_semaphore()
    for d in range(1, M):
        pl.semaphore_signal(barrier, inc=1, device_id=(lax.rem(me + d, M), tile),
                            device_id_type=pl.DeviceIdType.MESH)
    for d in range(1, T):
        pl.semaphore_signal(barrier, inc=1, device_id=(me, lax.rem(tile + d, T)),
                            device_id_type=pl.DeviceIdType.MESH)

    loads = [
        pltpu.make_async_copy(src, dst, in_sem.at[k])
        for k, (src, dst) in enumerate([
            (coarse_h, xin.at[HALO:HALO + R]), (kin_h, kin), (bank_h, bank), (cond_h, cond),
            (offset_h, offset), (head_h, headt), (kmid_h, kmid), (kout_h, kout),
            (target_h, target),
        ])
    ]
    for cp in loads:
        cp.start()

    for cp in loads[1:6]:
        cp.wait()
    for i in range(3):
        for j in range(3):
            kcat[V * i:V * (i + 1), C * j:C * (j + 1)] = kin[3 * i + j]
    lane = lax.broadcasted_iota(jnp.int32, bank.shape, 1)
    latent = []
    for m in range(mm):
        noise = jnp.sum(jnp.where(lane == seeds[m], bank[...], 0.0), axis=1, keepdims=True)
        latent.append(jnp.sum(noise * cond[...], axis=0, keepdims=True))
    rows8 = rfac.shape[0]
    row = lax.broadcasted_iota(jnp.int32, (rows8, 128), 0) + (band[0] + tile * R)
    lat = math.pi * (row.astype(F32) + 0.5) / GRID_ROWS - math.pi / 2
    rfac[...] = jnp.cos(lat) / (T * R * W)
    eye = lax.broadcasted_iota(jnp.int32, (V, V), 0) == lax.broadcasted_iota(jnp.int32, (V, V), 1)
    off_col = jnp.sum(jnp.where(eye, jnp.broadcast_to(offset[...], (V, V)), 0.0), axis=1,
                      keepdims=True)
    acc[0:E, :] = jnp.zeros((E, C), F32)

    pl.semaphore_wait(barrier, (M - 1) + (T - 1))

    down = remote(coarse_h.at[R - HALO:R], xin.at[0:HALO], halo_send.at[0], halo_recv.at[0],
                  me, lax.rem(tile + 1, T))
    up = remote(coarse_h.at[0:HALO], xin.at[HALO + R:2 * HALO + R], halo_send.at[1],
                halo_recv.at[1], me, lax.rem(tile + T - 1, T))

    @pl.when(tile < T - 1)
    def _():
        down.start()

    @pl.when(tile > 0)
    def _():
        up.start()

    loads[0].wait()

    @pl.when(tile > 0)
    def _():
        down.wait_recv()

    @pl.when(tile < T - 1)
    def _():
        up.wait_recv()

    @pl.when(tile == 0)
    def _():
        xin[0:HALO] = jnp.zeros((HALO, V, W), BF16)

    @pl.when(tile == T - 1)
    def _():
        xin[HALO + R:2 * HALO + R] = jnp.zeros((HALO, V, W), BF16)

    def shift_down(x):
        w = lax.broadcasted_iota(jnp.int32, x.shape, 0)
        return jnp.where(w == 0, 0.0, pltpu.roll(x, 1, 0))

    def shift_up(x):
        w = lax.broadcasted_iota(jnp.int32, x.shape, 0)
        return jnp.where(w == W - 1, 0.0, pltpu.roll(x, W - 1, 0))

    def put_shifted(dst, m, q, x):
        dst[m, q, :, 0:C] = shift_down(x).astype(BF16)
        dst[m, q, :, C:2 * C] = x.astype(BF16)
        dst[m, q, :, 2 * C:3 * C] = shift_up(x).astype(BF16)

    def inside(grow):
        return jnp.logical_and(grow >= 0, grow < T * R)

    def rows(count, body):
        step = max(k for k in (1, 2, 3, 4) if count % k == 0)
        if step == count:
            for k in range(count):
                body(k, 0)
            return

        def several(q, carry):
            for k in range(step):
                body(q * step + k, carry)
            return carry

        lax.fori_loop(0, count // step, several, 0)

    def first_row(q, carry):
        p = dot(xin[pl.ds(q, 3)].reshape(3 * V, W), kcat[...], 0, 0)
        base = shift_down(p[:, 0:C]) + p[:, C:2 * C] + shift_up(p[:, 2 * C:3 * C])
        centred = base - jnp.mean(base, axis=-1, keepdims=True)
        spread = jnp.mean(centred * centred, axis=-1, keepdims=True)
        normed = centred * lax.rsqrt(spread + 1e-05)
        ok = inside(tile * R + q - 2)
        for m in range(mm):
            mixed = normed * (1.0 + latent[m][:, 0:C]) + latent[m][:, C:2 * C]
            put_shifted(s1, m, q, jnp.where(ok, gelu(mixed), 0.0))
        return carry

    rows(R + 4, first_row)
    loads[6].wait()
    loads[7].wait()

    def fc_copy(m, d, slot):
        return remote(fc.at[slot], fc.at[slot], fc_send.at[m, d - 1], fc_recv.at[m, d - 1],
                      lax.rem(me + d, M), tile)

    for m in range(mm):
        def second_row(q, carry, m=m):
            h = dot(s1[m, q], kmid[0], 1, 0)
            h = h + dot(s1[m, q + 1], kmid[1], 1, 0)
            h = h + dot(s1[m, q + 2], kmid[2], 1, 0)
            put_shifted(s2, m, q, jnp.where(inside(tile * R + q - 1), gelu(h), 0.0))
            return carry

        rows(R + 2, second_row)
        slot = me * mm + m

        def out_row(r, carry, m=m, slot=slot):
            h = dot(s2[m, r], kout[0], 1, 0)
            h = h + dot(s2[m, r + 1], kout[1], 1, 0)
            h = h + dot(s2[m, r + 2], kout[2], 1, 0)
            g, s = gelu_and_slope(h)
            slope[m, r] = s
            feat = (s1[m, r + 2, :, C:2 * C].astype(F32) + g).astype(BF16)
            third[m, r] = feat
            f = dot(headt[...], feat, 1, 1) + xin[HALO + r].astype(F32) + off_col
            fc[slot, r] = f.astype(BF16)
            return carry

        rows(R, out_row)
        for d in range(1, M):
            fc_copy(m, d, slot).start()

    loads[8].wait()
    for m in range(mm):
        for d in range(1, M):
            fc_copy(m, d, lax.rem(me + M - d, M) * mm + m).wait_recv()

    def cot_row(r, carry):
        truth = target[r].astype(F32)
        factor = rfac[pl.ds(r, 1), 0:1]
        for m in range(mm):
            f = fc[me * mm + m, r].astype(F32)
            s = jnp.zeros_like(f)
            for j in range(members):
                s = s + sign(f - fc[j, r].astype(F32))
            c = factor * (sign(f - truth) / members - s / (members * (members - 1)))
            cb = c.astype(BF16)
            cot[m, r] = cb
            back = dot(cb, headt[...], 0, 0)
            dpre[m, r] = (back * slope[m, r]).astype(BF16)
            acc[0:V, :] += dot(cb, third[m, r], 1, 0)
            acc[V:V + 8, 0:V] += dot(jnp.ones((8, W), BF16), cb, 1, 1)
        return carry

    rows(R, cot_row)

    mate = me + 1 - 2 * core
    sizes_b = (E, 3 * C, 3 * C, 3 * C)

    def mine(b, c, x, part):
        first = sum(sizes_b[:b]) + c * (sizes_b[b] // 2) + x * (sizes_b[b] // M)
        return pl.ds(pl.multiple_of(first, 8), part)

    def c_copy(b):
        h = sizes_b[b] // 2
        at = sum(sizes_b[:b]) // 2
        return remote(acc.at[mine(b, 1 - core, 0, h)], rc.at[at:at + h], c_send.at[b],
                      c_recv.at[b], mate, tile)

    def x_copy(b, d):
        part = sizes_b[b] // M
        at = sum(sizes_b[:b]) // M
        to = lax.rem(xi + d, X)
        return remote(acc.at[mine(b, core, to, part)], rx.at[d - 1, at:at + part],
                      x_send.at[d - 1, b], x_recv.at[d - 1, b], to * 2 + core, tile)

    def core_sum(b):
        h = sizes_b[b] // 2
        at = sum(sizes_b[:b]) // 2
        c_copy(b).wait_recv()
        acc[mine(b, core, 0, h), :] += rc[at:at + h]
        for d in range(1, X):
            x_copy(b, d).start()

    def chunk_sum(b):
        part = sizes_b[b] // M
        at = sum(sizes_b[:b]) // M
        own = acc[mine(b, core, xi, part), :]
        for d in range(1, X):
            x_copy(b, d).wait_recv()
            own = own + rx[d - 1, at:at + part]
        quarter[at:at + part, :] = own

    c_copy(0).start()
    for i in range(3):
        g = jnp.zeros((3 * C, C), F32)
        for m in range(mm):
            g = g + dot(s2[m, i:i + R].reshape(R * W, 3 * C), dpre[m].reshape(R * W, C), 0, 0)
        acc[E + 3 * C * i:E + 3 * C * (i + 1), :] = g
        c_copy(i + 1).start()
        core_sum(i)

    def crps_row(r, carry):
        truth = target[r].astype(F32)
        fs = [fc[j, r].astype(F32) for j in range(members)]
        near = jnp.zeros_like(truth)
        pair = jnp.zeros_like(truth)
        for i in range(members):
            near = near + jnp.abs(fs[i] - truth)
            for j in range(i + 1, members):
                pair = pair + jnp.abs(fs[i] - fs[j])
        score[r] = near / members - (2.0 * pair) / (2 * members * (members - 1))
        return carry

    core_sum(3)
    rows(R, crps_row)
    share = V // M
    for k in range(M):
        @pl.when(me == k)
        def _(k=k):
            crps[...] = score[:, share * k:share * (k + 1), :]

    for b in range(4):
        chunk_sum(b)

    half, chunk, piece = X * per, per, per // T

    def t_at(x, t):
        return pl.multiple_of(core * half + x * chunk + t * piece, 8)

    ts = []
    for d in range(1, T):
        to = lax.rem(tile + d, T)
        ts.append(remote(quarter.at[pl.ds(pl.multiple_of(to * piece, 8), piece)], rt.at[d - 1], t_send.at[d - 1],
                         t_recv.at[d - 1], me, to))
    for cp in ts:
        cp.start()
    own = quarter[pl.ds(pl.multiple_of(tile * piece, 8), piece), :]
    for d in range(1, T):
        ts[d - 1].wait_recv()
        own = own + rt[d - 1]
    total[pl.ds(t_at(xi, tile), piece), :] = own

    def here(x, t):
        return total.at[pl.ds(t_at(x, t), piece)]

    def gt_copy(d, t):
        return remote(here(xi, t), here(xi, t), gt_send.at[d - 1], gt_recv.at[d - 1],
                      me, lax.rem(tile + d, T))

    def gx_copy(d, k, x, t):
        return remote(here(x, t), here(x, t), gx_send.at[d - 1, k], gx_recv.at[d - 1, k],
                      lax.rem(xi + d, X) * 2 + core, tile)

    def gc_copy(d, k, x, t, c):
        at = pl.multiple_of(c * half + x * chunk + t * piece, 8)
        ref = total.at[pl.ds(at, piece)]
        return remote(ref, ref, gc_send.at[d, k], gc_recv.at[d, k], mate, tile)

    for d in range(1, T):
        gt_copy(d, tile).start()
    for k in range(T):
        t = lax.rem(tile + T - k, T)
        if k > 0:
            gt_copy(k, t).wait_recv()
        for d in range(1, X):
            gx_copy(d, k, xi, t).start()
        gc_copy(0, k, xi, t, core).start()
    for k in range(T):
        t = lax.rem(tile + T - k, T)
        for d in range(1, X):
            x = lax.rem(xi + X - d, X)
            gx_copy(d, k, x, t).wait_recv()
            gc_copy(d, k, x, t, core).start()
    for k in range(T):
        t = lax.rem(tile + T - k, T)
        for d in range(X):
            gc_copy(d, k, lax.rem(xi + X - d, X), t, 1 - core).wait_recv()

    extra, part = E // M, 3 * C // M
    for q in range(M):
        for i in range(3):
            at = per * q + extra + part * i
            cgrad[3 * C * i + part * q:3 * C * i + part * (q + 1), :] = total[at:at + part, :]
    hgrad[...] = total[0:V, :]
    at = per * (V // extra) + V % extra
    bgrad[...] = total[at:at + 1, 0:V]

    @pl.when(tile < T - 1)
    def _():
        down.wait_send()

    @pl.when(tile > 0)
    def _():
        up.wait_send()

    for m in range(mm):
        for d in range(1, M):
            fc_copy(m, d, me * mm + m).wait_send()
    for b in range(4):
        c_copy(b).wait_send()
        for d in range(1, X):
            x_copy(b, d).wait_send()
    for cp in ts:
        cp.wait_send()
    for d in range(1, T):
        gt_copy(d, tile).wait_send()
    for k in range(T):
        t = lax.rem(tile + T - k, T)
        for d in range(1, X):
            gx_copy(d, k, xi, t).wait_send()
        for d in range(X):
            gc_copy(d, k, lax.rem(xi + X - d, X), t, core).wait_send()


def on_device(coarse, target, seeds, band, bank, cond, kin, kmid, kout, head, offset):
    M, T = lax.axis_size("member"), lax.axis_size("tile")
    mm = seeds.shape[0]
    R, V, W = coarse.shape
    C = kmid.shape[3]
    extra = -(-V // 8) * 8
    while (9 * C // M + extra) % (8 * T) or extra * M < V + 8:
        extra += 8
    E, per = extra * M, 9 * C // M + extra
    N = per * M
    X = M // 2
    sizes = (M, T, mm, R, V, W, C, E, per)
    vmem = pl.BlockSpec(memory_space=pltpu.VMEM)
    smem = pl.BlockSpec(memory_space=pltpu.SMEM)
    dma = pltpu.SemaphoreType.DMA
    scratch = [
        pltpu.VMEM((9, V, C), BF16),
        pltpu.VMEM(bank.shape[::-1], F32),
        pltpu.VMEM(cond.shape, F32),
        pltpu.VMEM((1, V), F32),
        pltpu.VMEM((V, C), BF16),
        pltpu.VMEM((3, 3 * C, C), BF16),
        pltpu.VMEM((3, 3 * C, C), BF16),
        pltpu.VMEM((R, V, W), BF16),
        dma((9,)),
        pltpu.VMEM((R + 2 * HALO, V, W), BF16),
        pltpu.VMEM((3 * V, 3 * C), BF16),
        pltpu.VMEM((mm, R + 4, W, 3 * C), BF16),
        pltpu.VMEM((mm, R + 2, W, 3 * C), BF16),
        pltpu.VMEM((mm, R, W, C), BF16),
        pltpu.VMEM((mm, R, W, C), F32),
        pltpu.VMEM((mm, R, W, C), BF16),
        pltpu.VMEM((M * mm, R, V, W), BF16),
        pltpu.VMEM((mm, R, V, W), BF16),
        pltpu.VMEM((-(-R // 8) * 8, 128), F32),
        pltpu.VMEM((R, V, W), F32),
        pltpu.VMEM((N, C), F32),
        pltpu.VMEM((N // 2, C), F32),
        pltpu.VMEM((max(X - 1, 1), per, C), F32),
        pltpu.VMEM((per, C), F32),
        pltpu.VMEM((T - 1, N // (M * T), C), F32),
        pltpu.VMEM((N, C), F32),
        dma((2,)), dma((2,)), dma((mm, M - 1)), dma((mm, M - 1)),
        dma((4,)), dma((4,)), dma((max(X - 1, 1), 4)), dma((max(X - 1, 1), 4)), dma((T - 1,)), dma((T - 1,)),
        dma((T - 1,)), dma((T - 1,)), dma((max(X - 1, 1), T)), dma((max(X - 1, 1), T)),
        dma((X, T)), dma((X, T)),
    ]
    crps, cgrad, hgrad, bgrad = pl.pallas_call(
        functools.partial(kernel, sizes),
        out_shape=(
            jax.ShapeDtypeStruct((R, V // M, W), F32),
            jax.ShapeDtypeStruct((9 * C, C), F32),
            jax.ShapeDtypeStruct((V, C), F32),
            jax.ShapeDtypeStruct((1, V), F32),
        ),
        in_specs=[smem, smem] + [pl.BlockSpec(memory_space=pltpu.HBM)] * 9,
        out_specs=(vmem,) * 4,
        scratch_shapes=scratch,
        compiler_params=pltpu.CompilerParams(
            collective_id=0, has_side_effects=True, vmem_limit_bytes=48 * 1024 * 1024
        ),
    )(
        seeds, band, *(pltpu.with_memory_space_constraint(z, pltpu.HBM) for z in (coarse, kin.reshape(9, V, C), bank.T, cond, offset.reshape(1, V), head.T,
        kmid.reshape(3, 3 * C, C), kout.reshape(3, 3 * C, C), target)),
    )
    return crps, cgrad.reshape(3, 3, C, C), hgrad.T, bgrad.reshape(V)


def solution(mesh):
    return jax.shard_map(
        on_device,
        mesh=mesh,
        in_specs=(P("tile", None, None), P("tile", None, None), P("member")) + (P(),) * 8,
        out_specs=(P("tile", "member", None), P(), P(), P()),
        check_vma=False,
    )
```
